256 devices in a mesh: gx: 32 (over x, z), gy: 8 (over y, core).
Axes of the slice: x: 4, y: 4, z: 8, core: 2. Of those that a mesh axis runs over, the one named last changes fastest.
Arguments:
- ensemble: float32 [64, 2048, 2048], P('gx', None, 'gy'), may hold values from -6 to 6
- obs_values: float32 [4, 128], replicated, may hold values from -6 to 6
- obs_error: float32 [4, 128], replicated, may hold values from 0.3 to 3
- tile_weight: float32 [4, 128, 32, 8], P(None, None, 'gx', 'gy'), may hold values from 0.2 to 1
- owner_device: int32 [4], replicated, may hold values from 0 to 255
- obs_cells: int32 [4, 128], replicated, may hold values from 0 to 16383
Outputs:
- analysis_ensemble: float32 [64, 2048, 2048], P('gx', None, 'gy')
The draws below stay inside these ranges and needn't reach their ends.
Inputs may be any that keep to these rules, and one draw needn't show every extreme that they name: `owner_device`: device numbers count gy fastest: the device at index i of gx and j of gy is number i times the length of gy plus j. `obs_cells`: cell c of a tile lies c // 256 cells along the first direction and c % 256 along the second from the tile's first cell; cells may repeat.
All inputs are finite; a program needn't handle non-finite values.
Results may differ from the reference program's by a relative error of at most 0.00015.
Values sent between devices are 32-bit elements; how exact they have to be, the bound alone decides.
A program may use at most 64 MiB of HBM per device.

```python
import math
import jax
import jax.numpy as jnp
from jax import lax

VX = 64
VY = 256
NB = 4
NOBS = 128
MEMBERS = 64
NVX = 2048
NVY = 2048
REACH = 512
N_GX = 32
N_GY = 8


def touch_ends(values, stream_key, smallest, high):
    index_at = [jax.random.randint(jax.random.fold_in(stream_key, axis), (), 0, length) for axis, length in enumerate(values.shape)]
    longest = values.shape.index(max(values.shape))
    neighbour = index_at[:longest] + [(index_at[longest] + 1) % values.shape[longest]] + index_at[longest + 1:]
    return values.at[tuple(index_at)].set(smallest).at[tuple(neighbour)].set(high)


def block_scale(stream_key, shape, pieces, low, high):
    gain, own = 1.0, jax.random.fold_in(stream_key, 6)
    for axis_at, blocks in pieces:
        draws = jnp.exp(jax.random.uniform(jax.random.fold_in(own, axis_at), (blocks,), jnp.float32, low / len(pieces), high / len(pieces)))
        gain = gain * jnp.repeat(draws, shape[axis_at] // blocks).reshape([-1 if axis == axis_at else 1 for axis in range(len(shape))])
    return gain


def normal_values(key, extent, scale, limit, cuts=(), kind=jnp.bfloat16):
    array = scale * jax.random.normal(key, extent, jnp.float32)
    if cuts:
        array = array * block_scale(key, extent, cuts, -0.22, 0.18)
    return jnp.clip(array, -limit, limit).astype(kind)


def setup_inputs(seed: int = 0) -> dict:
    splits = jax.random.split(jax.random.key(seed), 7)
    return {
        "ensemble": normal_values(splits[0], (MEMBERS, NVX, NVY), 1.0, 6.0, ((0, 32), (2, 8)), jnp.float32),
        "obs_values": normal_values(splits[1], (NB, NOBS), 1.0, 6.0, (), jnp.float32),
        "obs_error": jnp.clip(jnp.exp(jax.random.uniform(splits[2], (NB, NOBS), jnp.float32, math.log(0.3), math.log(3.0))), 0.3, 3.0),
        "tile_weight": jnp.clip(0.2 + 0.8 * jax.random.uniform(splits[3], (NB, NOBS, N_GX, N_GY), jnp.float32) ** block_scale(splits[3], (NB, NOBS, N_GX, N_GY), ((2, 32), (3, 8)), -0.2, 0.2), 0.2, 1.0),
        "owner_device": touch_ends(jax.random.randint(splits[4], (NB,), 0, N_GX * N_GY), jax.random.fold_in(splits[4], 1), 0, (N_GX * N_GY) - 1).astype(jnp.int32),
        "obs_cells": touch_ends(jax.random.randint(splits[5], (NB, NOBS), 0, VX * VY), jax.random.fold_in(splits[5], 1), 0, (VX * VY) - 1).astype(jnp.int32),
    }


EPSILON = 1e-06
PRECISE = lax.Precision.HIGHEST

def analysis(prior_ens, values, errors):
    members = prior_ens.shape[1]
    average = lax.optimization_barrier(jnp.mean(prior_ens, axis=1, keepdims=True))
    anomaly = prior_ens - average
    spread = lax.optimization_barrier(jnp.sum(anomaly * anomaly, axis=1, keepdims=True)) / (members - 1) + EPSILON
    obs_noise = errors[:, None]
    post_var = 1.0 / (1.0 / spread + 1.0 / obs_noise)
    post_mean = post_var * (average / spread + values[:, None] / obs_noise)
    increment = post_mean - average + (jnp.sqrt(post_var / spread) - 1.0) * anomaly
    return (anomaly, spread, increment)

def regression(state_cols, anomaly, spread, increment, weight_cols, obs_xpos, obs_ypos, grid_xpos, grid_ypos, radius):
    members = state_cols.shape[0]
    deviation = state_cols - lax.optimization_barrier(jnp.mean(state_cols, axis=0, keepdims=True))
    covariance = jnp.dot(anomaly, deviation, precision=PRECISE) / (members - 1)
    distance = (grid_xpos[None, :] - obs_xpos[:, None]) ** 2 + (grid_ypos[None, :] - obs_ypos[:, None]) ** 2
    tapering = 1.0 / (1.0 + distance / radius)
    gain_rows = covariance * (tapering * weight_cols) / spread
    return state_cols + jnp.dot(increment.T, gain_rows, precision=PRECISE)

def reference(ensemble, obs_values, obs_error, tile_weight, owner_device, obs_cells):
    current = ensemble
    radius = float(REACH * REACH)
    cell_ids = jnp.arange(VX * NVY, dtype=jnp.int32)
    for batch in range(NB):
        owner_now = owner_device[batch]
        observed = obs_cells[batch]
        obs_gridx = owner_now // N_GY * VX + observed // VY
        obs_gridy = owner_now % N_GY * VY + observed % VY
        prior_ens = current[:, obs_gridx, obs_gridy].T
        anomaly, spread, increment = analysis(prior_ens, obs_values[batch], obs_error[batch])
        obs_xpos = obs_gridx.astype(jnp.float32)
        obs_ypos = obs_gridy.astype(jnp.float32)
        weights = tile_weight[batch]
        blocks = current.reshape(MEMBERS, N_GX, VX, NVY).transpose(1, 0, 2, 3)

        def update_block(element):
            x_block, column = element
            grid_xpos = (column * VX + cell_ids // NVY).astype(jnp.float32)
            grid_ypos = (cell_ids % NVY).astype(jnp.float32)
            stripe = jnp.repeat(weights[:, column, :], VY, axis=1)
            weight_cols = jnp.tile(stripe, (1, VX))
            state_cols = x_block.reshape(MEMBERS, VX * NVY)
            updated = regression(state_cols, anomaly, spread, increment, weight_cols, obs_xpos, obs_ypos, grid_xpos, grid_ypos, radius)
            return updated.reshape(MEMBERS, VX, NVY)
        updated = lax.map(update_block, (blocks, jnp.arange(N_GX, dtype=jnp.int32)))
        current = updated.transpose(1, 0, 2, 3).reshape(MEMBERS, NVX, NVY)
    return current
```

```python
import functools

import jax
import jax.numpy as jnp
from jax import lax
from jax.experimental import pallas as pl
from jax.experimental.pallas import tpu as pltpu
from jax.sharding import PartitionSpec as P

MESH = pl.DeviceIdType.MESH
EPSILON = 1e-06
F32 = jnp.float32
BF16 = jnp.bfloat16
HI = lax.Precision.HIGHEST
CH = 8
GROUP = 4
PAIRS = ((0, 1, 4), (0, 2, 5), (0, 3, 6), (1, 2, 12), (1, 3, 13), (2, 3, 14))


def split(a):
    hi = a.astype(BF16)
    return hi, (a - hi.astype(F32)).astype(BF16)


def kernel(
    dims,
    owner_s,
    cells_s,
    cells_v,
    values_v,
    errors_v,
    weight_v,
    ens,
    out,
    recv,
    stage,
    pay,
    gyb,
    pay2,
    gxb,
    xobs,
    a_tab,
    i_tab,
    t_tab,
    o_tab,
    gy_s,
    gy_r,
    gx_s,
    gx_r,
    in_s,
    in_r,
    in_l,
    out_s,
    out_r,
    out_l,
):
    nx, ny, members, rows, cols, nb, nobs = dims
    chunks = rows // CH
    sides = cols // 128
    reach = float(rows * nx // 4)
    gx = lax.axis_index("gx")
    gy = lax.axis_index("gy")
    px = gx // 8
    pz = lax.rem(gx, 8)

    def partner(q):
        t = q // 4
        hop = (t + 1) // 2
        dz = jnp.where(lax.rem(t, 2) == 1, hop, 8 - hop)
        return lax.rem(px + lax.rem(q, 4), 4) * 8 + lax.rem(pz + dz, 8)

    barrier = pltpu.get_barrier_semaphore()

    def greet_x(q, c):
        pl.semaphore_signal(
            barrier, inc=1, device_id=(lax.rem(gx + q, nx), gy), device_id_type=MESH
        )
        return c

    def greet_y(q, c):
        pl.semaphore_signal(
            barrier, inc=1, device_id=(gx, lax.rem(gy + q, ny)), device_id_type=MESH
        )
        return c

    lax.fori_loop(1, ny, greet_y, 0)
    lax.fori_loop(1, nx, greet_x, 0)

    lane = lax.broadcasted_iota(jnp.int32, (nobs, 128), 1)
    cells = cells_v[...]
    cx = cells // cols
    cy = cells - cx * cols
    ox_rows, oy_rows = [], []
    for b in range(nb):
        io = owner_s[b] // ny
        jo = owner_s[b] - io * ny
        ox_rows.append((cx[b : b + 1] + io * rows).astype(F32) * (1.0 / reach))
        oy_rows.append((cy[b : b + 1] + jo * cols).astype(F32) * (1.0 / reach))
    table = jnp.concatenate(
        ox_rows + oy_rows + [(cy - cy // 128 * 128).astype(F32), jnp.zeros((nobs - 3 * nb, nobs), F32)], axis=0
    )
    table_t = table.T

    lane_pos = lane.astype(F32)
    for b in range(nb):
        base = (owner_s[b] // ny) * rows

        def fetch(k, c, b=b, base=base):
            cell = cells_s[b, k]
            row = base + cell // cols
            side = lax.rem(cell, cols) // 128
            for m in range(2):
                stage[m, pl.ds(b * nobs + k, 1), :] = ens[
                    m, row // CH, side, pl.ds(lax.rem(row, CH), 1), :
                ]
            return c

        lax.fori_loop(0, nobs, fetch, 0, unroll=8)
    picked = jnp.zeros((nobs, 128), F32)
    for b in range(nb):
        hit = lane_pos == table_t[:, 2 * nb + b : 2 * nb + b + 1]
        mine = (owner_s[b] - (owner_s[b] // ny) * ny == gy).astype(F32)
        for m in range(2):
            rows_here = stage[m, b * nobs : (b + 1) * nobs, :]
            col = jnp.sum(jnp.where(hit, rows_here, 0.0), axis=1, keepdims=True) * mine
            picked = jnp.where(lane == m * 8 + b, col, picked)
    packet = picked.T[:16]
    line = lax.broadcasted_iota(jnp.int32, (16, nobs), 0)
    for b, later, r in PAIRS:
        mine = (owner_s[later] == gx * ny + gy).astype(F32)
        packet = jnp.where(line == r, weight_v[b : b + 1, :] * mine, packet)
    pay[...] = packet
    gyb[gy] = packet

    pl.semaphore_wait(barrier, nx + ny - 2)

    def send_y(q, c):
        pltpu.make_async_remote_copy(
            src_ref=pay,
            dst_ref=gyb.at[gy],
            send_sem=gy_s,
            recv_sem=gy_r,
            device_id=(gx, lax.rem(gy + q, ny)),
            device_id_type=MESH,
        ).start()
        return c

    lax.fori_loop(1, ny, send_y, 0)

    def send_in(c, carry):
        def one(q, carry2):
            peer = partner(q)
            pltpu.make_async_remote_copy(
                src_ref=ens.at[:, peer * chunks + c],
                dst_ref=recv.at[c, pl.ds(gx * 2, 2)],
                send_sem=in_s.at[c],
                recv_sem=in_r.at[c],
                device_id=(peer, gy),
                device_id_type=MESH,
            ).start()
            return carry2

        lax.fori_loop(1, nx, one, 0)
        pltpu.make_async_copy(
            ens.at[:, gx * chunks + c],
            recv.at[c, pl.ds(gx * 2, 2)],
            in_l.at[c],
        ).start()
        return carry

    lax.fori_loop(0, 1, send_in, 0)

    pltpu.make_async_copy(gyb.at[pl.ds(0, ny - 1)], gyb.at[pl.ds(0, ny - 1)], gy_r).wait()
    pltpu.make_async_copy(gyb.at[pl.ds(0, ny - 1)], gyb.at[pl.ds(0, ny - 1)], gy_s).wait()
    packet = gyb[0]
    for j in range(1, ny):
        packet = packet + gyb[j]
    pay2[...] = packet
    gxb[pl.ds(pl.multiple_of(gx * 16, 16), 16), :] = packet

    def send_x(q, c):
        pltpu.make_async_remote_copy(
            src_ref=pay2,
            dst_ref=gxb.at[pl.ds(pl.multiple_of(gx * 16, 16), 16), :],
            send_sem=gx_s,
            recv_sem=gx_r,
            device_id=(partner(q), gy),
            device_id_type=MESH,
        ).start()
        return c

    lax.fori_loop(1, nx, send_x, 0)
    lax.fori_loop(1, chunks, send_in, 0)

    part = gxb.at[pl.ds(0, (nx - 1) * 16), :]
    pltpu.make_async_copy(part, part, gx_r).wait()
    pltpu.make_async_copy(part, part, gx_s).wait()

    for b in range(nb):
        xobs[:, b * nobs : (b + 1) * nobs] = gxb[pl.ds(b, members, stride=8), :]
    w_rows = [
        jnp.sum(gxb[pl.ds(r, nx, stride=16), :], axis=0, keepdims=True) for _, _, r in PAIRS
    ]
    w_t = jnp.concatenate(w_rows + [jnp.zeros((nobs - len(PAIRS), nobs), F32)], axis=0).T

    y_here = (
        lax.broadcasted_iota(jnp.int32, (nobs, cols), 1) + gy * cols
    ).astype(F32) * (1.0 / reach)
    for b in range(nb):
        prior = xobs[:, b * nobs : (b + 1) * nobs]
        average = jnp.mean(prior, axis=0, keepdims=True)
        anomaly = prior - average
        spread = jnp.sum(anomaly * anomaly, axis=0, keepdims=True) / (members - 1) + EPSILON
        noise = errors_v[b : b + 1, :]
        post_var = 1.0 / (1.0 / spread + 1.0 / noise)
        post_mean = post_var * (average / spread + values_v[b : b + 1, :] / noise)
        increment = post_mean - average + (jnp.sqrt(post_var / spread) - 1.0) * anomaly
        scaled = anomaly * (1.0 / ((members - 1) * spread))
        ox = table_t[:, b : b + 1]
        oy = table_t[:, nb + b : nb + b + 1]
        if b < nb - 1:
            later = xobs[:, (b + 1) * nobs :]
            deviation = later - jnp.mean(later, axis=0, keepdims=True)
            cov = jnp.dot(scaled.T, deviation, precision=HI, preferred_element_type=F32)
            gains = []
            for later_b in range(b + 1, nb):
                dx = table[later_b : later_b + 1] - ox
                dy = table[nb + later_b : nb + later_b + 1] - oy
                n = [p[:2] for p in PAIRS].index((b, later_b))
                taper = w_t[:, n : n + 1] / (1.0 + (dx * dx + dy * dy))
                at = (later_b - b - 1) * nobs
                gains.append(cov[:, at : at + nobs] * taper)
            gain = jnp.concatenate(gains, axis=1)
            xobs[:, (b + 1) * nobs :] = later + jnp.dot(
                increment, gain, precision=HI, preferred_element_type=F32
            )
        a_hi, a_lo = split((scaled * weight_v[b : b + 1, :]).T)
        a_tab[b] = jnp.concatenate([a_hi, a_lo, a_hi, a_lo], axis=1)
        i_hi, i_lo = split(increment)
        i_tab[b] = jnp.concatenate(
            [jnp.concatenate([i_hi, i_hi], axis=1), jnp.concatenate([i_lo, i_lo], axis=1)],
            axis=0,
        )
        dy = y_here - oy
        t_tab[b] = 1.0 + dy * dy
        o_tab[b] = jnp.broadcast_to(ox, (nobs, 128))

    def work(c, carry):
        some = recv.at[c, pl.ds(0, 2 * (nx - 1))]
        pltpu.make_async_copy(some, some, in_r.at[c]).wait()
        own = recv.at[c, pl.ds(gx * 2, 2)]
        pltpu.make_async_copy(own, own, in_l.at[c]).wait()
        flat = recv.at[c].reshape(members * sides * CH, 128)

        def group(g, carry2):
            first = g * GROUP
            x = jnp.concatenate(
                [
                    flat[pl.ds(first + r + h * CH, members, stride=sides * CH), :]
                    for r in range(GROUP)
                    for h in range(sides)
                ],
                axis=1,
            )
            for b in range(nb):
                deviation = x - jnp.mean(x, axis=0, keepdims=True)
                d_hi, d_lo = split(deviation)
                cov = jnp.dot(
                    a_tab[b],
                    jnp.concatenate([d_hi, d_hi, d_lo, d_lo], axis=0),
                    preferred_element_type=F32,
                )
                gains = []
                for r in range(GROUP):
                    x_here = (gx * rows + c * CH + first + r).astype(F32) * (1.0 / reach)
                    dx = x_here - o_tab[b]
                    dx = dx * dx
                    far = t_tab[b] + jnp.concatenate([dx] * sides, axis=1)
                    gains.append(cov[:, r * cols : (r + 1) * cols] / far)
                g_hi, g_lo = split(jnp.concatenate(gains, axis=1))
                change = jnp.dot(
                    i_tab[b],
                    jnp.concatenate([g_hi, g_lo], axis=0),
                    preferred_element_type=F32,
                )
                x = x + (change[:members] + change[members:])
            for r in range(GROUP):
                for h in range(sides):
                    at = r * cols + h * 128
                    flat[pl.ds(first + r + h * CH, members, stride=sides * CH), :] = x[
                        :, at : at + 128
                    ]
            return carry2

        lax.fori_loop(0, CH // GROUP, group, 0)

        there = gx * chunks + c

        def one(q, carry2):
            peer = partner(q)
            pltpu.make_async_remote_copy(
                src_ref=recv.at[c, pl.ds(peer * 2, 2)],
                dst_ref=out.at[:, there],
                send_sem=out_s.at[c],
                recv_sem=out_r,
                device_id=(peer, gy),
                device_id_type=MESH,
            ).start()
            return carry2

        lax.fori_loop(1, nx, one, 0)
        pltpu.make_async_copy(
            recv.at[c, pl.ds(gx * 2, 2)], out.at[:, there], out_l.at[c]
        ).start()
        return carry

    lax.fori_loop(0, chunks, work, 0)

    def finish(c, carry):
        some = recv.at[c, pl.ds(0, 2 * (nx - 1))]
        pltpu.make_async_copy(some, some, in_s.at[c]).wait()
        pltpu.make_async_copy(some, some, out_s.at[c]).wait()
        there = out.at[:, gx * chunks + c]
        pltpu.make_async_copy(recv.at[c, pl.ds(gx * 2, 2)], there, out_l.at[c]).wait()
        return carry

    lax.fori_loop(0, chunks, finish, 0)
    rest = out.at[:, pl.ds(0, (nx - 1) * chunks)]
    pltpu.make_async_copy(rest, rest, out_r).wait()


def local(nx, ny, ensemble, obs_values, obs_error, tile_weight, owner_device, obs_cells):
    own, length, cols = ensemble.shape
    nb, nobs = obs_cells.shape
    members = own * nx
    rows = length // nx
    chunks = rows // CH
    dims = (nx, ny, members, rows, cols, nb, nobs)
    vmem = pl.BlockSpec(memory_space=pltpu.VMEM)
    smem = pl.BlockSpec(memory_space=pltpu.SMEM)
    dma = pltpu.SemaphoreType.DMA
    tiles = ensemble.reshape(own, length // CH, CH, cols // 128, 128).transpose(0, 1, 3, 2, 4)
    result = pl.pallas_call(
        functools.partial(kernel, dims),
        out_shape=jax.ShapeDtypeStruct(tiles.shape, F32),
        in_specs=[smem, smem, vmem, vmem, vmem, vmem, vmem],
        out_specs=pl.BlockSpec(memory_space=pl.ANY),
        scratch_shapes=[
            pltpu.VMEM((chunks, members, cols // 128, CH, 128), F32),
            pltpu.VMEM((2, nb * nobs, 128), F32),
            pltpu.VMEM((16, nobs), F32),
            pltpu.VMEM((ny, 16, nobs), F32),
            pltpu.VMEM((16, nobs), F32),
            pltpu.VMEM((nx * 16, nobs), F32),
            pltpu.VMEM((members, nb * nobs), F32),
            pltpu.VMEM((nb, nobs, 4 * members), BF16),
            pltpu.VMEM((nb, 2 * members, 2 * nobs), BF16),
            pltpu.VMEM((nb, nobs, cols), F32),
            pltpu.VMEM((nb, nobs, 128), F32),
            dma,
            dma,
            dma,
            dma,
            dma((chunks,)),
            dma((chunks,)),
            dma((chunks,)),
            dma((chunks,)),
            dma,
            dma((chunks,)),
        ],
        compiler_params=pltpu.CompilerParams(
            collective_id=0, has_side_effects=True, vmem_limit_bytes=40 * 1024 * 1024
        ),
    )(
        owner_device,
        obs_cells,
        obs_cells,
        obs_values,
        obs_error,
        tile_weight.reshape(nb, nobs),
        tiles,
    )
    return result.transpose(0, 1, 3, 2, 4).reshape(ensemble.shape)


def solution(mesh):
    placed = (P("gx", None, "gy"), P(), P(), P(None, None, "gx", "gy"), P(), P())
    return jax.shard_map(
        functools.partial(local, mesh.shape["gx"], mesh.shape["gy"]),
        mesh=mesh,
        in_specs=placed,
        out_specs=P("gx", None, "gy"),
        check_vma=False,
    )
```

```python
import functools

import jax
import jax.numpy as jnp
from jax import lax
from jax.experimental import pallas as pl
from jax.experimental.pallas import tpu as pltpu
from jax.sharding import PartitionSpec as P

MESH = pl.DeviceIdType.MESH
EPSILON = 1e-06
F32 = jnp.float32
BF16 = jnp.bfloat16
HI = lax.Precision.HIGHEST
CH = 8
GROUP = 4
EARLY = 2
MIDDLE = 3
LATE = 4
PAIRS = ((0, 1), (0, 2), (0, 3), (1, 2), (1, 3), (2, 3))


def split(a):
    hi = a.astype(BF16)
    return hi, (a - hi.astype(F32)).astype(BF16)


def kernel(
    dims,
    owner_h,
    cells_h,
    values_h,
    errors_h,
    weight_h,
    ens_h,
    out,
    owner_s,
    cells_s,
    cells_v,
    values_v,
    errors_v,
    weight_v,
    ens,
    recv,
    stage,
    pay,
    gyb,
    gxb,
    xobs,
    a_tab,
    i_tab,
    t_tab,
    o_tab,
    gy_s,
    gy_r,
    gx_s,
    gx_r,
    all_s,
    all_r,
    in_s,
    in_r,
    in_l,
    out_s,
    out_r,
    out_l,
    load,
):
    nx, ny, members, rows, cols, nb, nobs = dims
    chunks = rows // CH
    sides = cols // 128
    reach = float(rows * nx // 4)
    gx = lax.axis_index("gx")
    gy = lax.axis_index("gy")
    px = gx // 8
    pz = lax.rem(gx, 8)

    def partner(q):
        t = q // 4
        hop = (t + 1) // 2
        dz = jnp.where(lax.rem(t, 2) == 1, hop, 8 - hop)
        return lax.rem(px + lax.rem(q, 4), 4) * 8 + lax.rem(pz + dz, 8)

    barrier = pltpu.get_barrier_semaphore()

    def greet_x(q, c):
        pl.semaphore_signal(
            barrier, inc=1, device_id=(lax.rem(gx + q, nx), gy), device_id_type=MESH
        )
        return c

    def greet_y(q, c):
        pl.semaphore_signal(
            barrier, inc=1, device_id=(gx, lax.rem(gy + q, ny)), device_id_type=MESH
        )
        return c

    lax.fori_loop(1, ny, greet_y, 0)
    lax.fori_loop(1, nx, greet_x, 0)

    loads = [
        pltpu.make_async_copy(src, dst, load.at[n])
        for n, (src, dst) in enumerate(
            (
                (owner_h, owner_s),
                (cells_h, cells_s),
                (cells_h, cells_v),
                (values_h, values_v),
                (errors_h, errors_v),
                (weight_h, weight_v),
                (ens_h, ens),
            )
        )
    ]
    for copy in loads:
        copy.start()

    def send_in(c, carry):
        def one(q, carry2):
            peer = partner(q)
            pltpu.make_async_remote_copy(
                src_ref=ens_h.at[:, peer * chunks + c],
                dst_ref=recv.at[c, pl.ds(gx * 2, 2)],
                send_sem=in_s.at[c],
                recv_sem=in_r.at[c],
                device_id=(peer, gy),
                device_id_type=MESH,
            ).start()
            return carry2

        lax.fori_loop(1, nx, one, 0)
        pltpu.make_async_copy(
            ens_h.at[:, gx * chunks + c], recv.at[c, pl.ds(gx * 2, 2)], in_l.at[c]
        ).start()
        return carry

    pl.semaphore_wait(barrier, nx + ny - 2)
    lax.fori_loop(0, EARLY, send_in, 0)
    for copy in loads:
        copy.wait()

    lane = lax.broadcasted_iota(jnp.int32, (nobs, 128), 1)
    cells = cells_v[...]
    cx = cells // cols
    cy = cells - cx * cols
    ox_rows, oy_rows = [], []
    for b in range(nb):
        io = owner_s[b] // ny
        jo = owner_s[b] - io * ny
        ox_rows.append((cx[b : b + 1] + io * rows).astype(F32) * (1.0 / reach))
        oy_rows.append((cy[b : b + 1] + jo * cols).astype(F32) * (1.0 / reach))
    table = jnp.concatenate(
        ox_rows + oy_rows + [(cy - cy // 128 * 128).astype(F32), jnp.zeros((nobs - 3 * nb, nobs), F32)], axis=0
    )
    table_t = table.T

    lane_pos = lane.astype(F32)
    for b in range(nb):
        base = (owner_s[b] // ny) * rows

        def fetch(k, c, b=b, base=base):
            cell = cells_s[b, k]
            row = base + cell // cols
            side = lax.rem(cell, cols) // 128
            for m in range(2):
                stage[m, pl.ds(b * nobs + k, 1), :] = ens[
                    m, row // CH, side, pl.ds(lax.rem(row, CH), 1), :
                ]
            return c

        lax.fori_loop(0, nobs, fetch, 0, unroll=8)
    picked = jnp.zeros((nobs, 128), F32)
    for b in range(nb):
        hit = lane_pos == table_t[:, 2 * nb + b : 2 * nb + b + 1]
        mine = (owner_s[b] - (owner_s[b] // ny) * ny == gy).astype(F32)
        for m in range(2):
            rows_here = stage[m, b * nobs : (b + 1) * nobs, :]
            col = jnp.sum(jnp.where(hit, rows_here, 0.0), axis=1, keepdims=True) * mine
            picked = jnp.where(lane == 2 * b + m, col, picked)
    packet = picked.T[:16]
    line = lax.broadcasted_iota(jnp.int32, (16, nobs), 0)
    for n, (b, later) in enumerate(PAIRS):
        mine = (owner_s[later] == gx * ny + gy).astype(F32)
        packet = jnp.where(line == 2 * nb + n, weight_v[b : b + 1, :] * mine, packet)
    pay[...] = packet
    for i in range(2):
        gyb[pl.ds(2 * gy + i, 1), :] = pay[pl.ds(2 * gy + i, 1), :]

    def send_y(q, c):
        peer = lax.rem(gy + q, ny)
        pltpu.make_async_remote_copy(
            src_ref=pay.at[pl.ds(2 * peer, 2), :],
            dst_ref=gyb.at[pl.ds(2 * gy, 2), :],
            send_sem=gy_s,
            recv_sem=gy_r,
            device_id=(gx, peer),
            device_id_type=MESH,
        ).start()
        return c

    lax.fori_loop(1, ny, send_y, 0)
    lax.fori_loop(EARLY, MIDDLE, send_in, 0)

    part = gyb.at[pl.ds(0, 2 * (ny - 1)), :]
    pltpu.make_async_copy(part, part, gy_r).wait()
    pltpu.make_async_copy(part, part, gy_s).wait()
    for i in range(2):
        gxb[gy, pl.ds(2 * gx + i, 1), :] = jnp.sum(
            gyb[pl.ds(i, ny, stride=2), :], axis=0, keepdims=True
        )

    def send_x(q, c):
        mine = gxb.at[gy, pl.ds(2 * gx, 2), :]
        pltpu.make_async_remote_copy(
            src_ref=mine,
            dst_ref=mine,
            send_sem=gx_s,
            recv_sem=gx_r,
            device_id=(partner(q), gy),
            device_id_type=MESH,
        ).start()
        return c

    lax.fori_loop(1, nx, send_x, 0)
    lax.fori_loop(MIDDLE, LATE, send_in, 0)
    part = gxb.at[0, pl.ds(0, 2 * (nx - 1)), :]
    pltpu.make_async_copy(part, part, gx_r).wait()
    pltpu.make_async_copy(part, part, gx_s).wait()

    def send_all(q, c):
        pltpu.make_async_remote_copy(
            src_ref=gxb.at[gy],
            dst_ref=gxb.at[gy],
            send_sem=all_s,
            recv_sem=all_r,
            device_id=(gx, lax.rem(gy + q, ny)),
            device_id_type=MESH,
        ).start()
        return c

    lax.fori_loop(1, ny, send_all, 0)
    lax.fori_loop(LATE, chunks, send_in, 0)
    part = gxb.at[pl.ds(0, ny - 1)]
    pltpu.make_async_copy(part, part, all_r).wait()
    pltpu.make_async_copy(part, part, all_s).wait()

    for b in range(nb):
        xobs[:, b * nobs : (b + 1) * nobs] = gxb[b]
    w_rows = [
        jnp.sum(gxb[nb + n // 2, pl.ds(n % 2, nx, stride=2), :], axis=0, keepdims=True)
        for n in range(len(PAIRS))
    ]
    w_t = jnp.concatenate(w_rows + [jnp.zeros((nobs - len(PAIRS), nobs), F32)], axis=0).T

    y_here = (
        lax.broadcasted_iota(jnp.int32, (nobs, cols), 1) + gy * cols
    ).astype(F32) * (1.0 / reach)
    for b in range(nb):
        prior = xobs[:, b * nobs : (b + 1) * nobs]
        average = jnp.mean(prior, axis=0, keepdims=True)
        anomaly = prior - average
        spread = jnp.sum(anomaly * anomaly, axis=0, keepdims=True) / (members - 1) + EPSILON
        noise = errors_v[b : b + 1, :]
        post_var = 1.0 / (1.0 / spread + 1.0 / noise)
        post_mean = post_var * (average / spread + values_v[b : b + 1, :] / noise)
        increment = post_mean - average + (jnp.sqrt(post_var / spread) - 1.0) * anomaly
        scaled = anomaly * (1.0 / ((members - 1) * spread))
        ox = table_t[:, b : b + 1]
        oy = table_t[:, nb + b : nb + b + 1]
        if b < nb - 1:
            later = xobs[:, (b + 1) * nobs :]
            deviation = later - jnp.mean(later, axis=0, keepdims=True)
            cov = jnp.dot(scaled.T, deviation, precision=HI, preferred_element_type=F32)
            gains = []
            for later_b in range(b + 1, nb):
                dx = table[later_b : later_b + 1] - ox
                dy = table[nb + later_b : nb + later_b + 1] - oy
                n = PAIRS.index((b, later_b))
                taper = w_t[:, n : n + 1] / (1.0 + (dx * dx + dy * dy))
                at = (later_b - b - 1) * nobs
                gains.append(cov[:, at : at + nobs] * taper)
            gain = jnp.concatenate(gains, axis=1)
            xobs[:, (b + 1) * nobs :] = later + jnp.dot(
                increment, gain, precision=HI, preferred_element_type=F32
            )
        a_hi, a_lo = split((scaled * weight_v[b : b + 1, :]).T)
        a_tab[b] = jnp.concatenate([a_hi, a_lo, a_hi, a_lo], axis=1)
        i_hi, i_lo = split(increment)
        i_tab[b] = jnp.concatenate(
            [jnp.concatenate([i_hi, i_hi], axis=1), jnp.concatenate([i_lo, i_lo], axis=1)],
            axis=0,
        )
        dy = y_here - oy
        t_tab[b] = 1.0 + dy * dy
        o_tab[b] = jnp.broadcast_to(ox, (nobs, 128))

    def work(c, carry):
        some = recv.at[c, pl.ds(0, 2 * (nx - 1))]
        pltpu.make_async_copy(some, some, in_r.at[c]).wait()
        own = recv.at[c, pl.ds(gx * 2, 2)]
        pltpu.make_async_copy(own, own, in_l.at[c]).wait()
        flat = recv.at[c].reshape(members * sides * CH, 128)

        def group(g, carry2):
            first = g * GROUP
            x = jnp.concatenate(
                [
                    flat[pl.ds(first + r + h * CH, members, stride=sides * CH), :]
                    for r in range(GROUP)
                    for h in range(sides)
                ],
                axis=1,
            )
            for b in range(nb):
                deviation = x - jnp.mean(x, axis=0, keepdims=True)
                d_hi, d_lo = split(deviation)
                cov = jnp.dot(
                    a_tab[b],
                    jnp.concatenate([d_hi, d_hi, d_lo, d_lo], axis=0),
                    preferred_element_type=F32,
                )
                gains = []
                for r in range(GROUP):
                    x_here = (gx * rows + c * CH + first + r).astype(F32) * (1.0 / reach)
                    dx = x_here - o_tab[b]
                    dx = dx * dx
                    far = t_tab[b] + jnp.concatenate([dx] * sides, axis=1)
                    gains.append(cov[:, r * cols : (r + 1) * cols] / far)
                g_hi, g_lo = split(jnp.concatenate(gains, axis=1))
                change = jnp.dot(
                    i_tab[b],
                    jnp.concatenate([g_hi, g_lo], axis=0),
                    preferred_element_type=F32,
                )
                x = x + (change[:members] + change[members:])
            for r in range(GROUP):
                for h in range(sides):
                    at = r * cols + h * 128
                    flat[pl.ds(first + r + h * CH, members, stride=sides * CH), :] = x[
                        :, at : at + 128
                    ]
            return carry2

        lax.fori_loop(0, CH // GROUP, group, 0)

        there = gx * chunks + c

        def one(q, carry2):
            peer = partner(q)
            pltpu.make_async_remote_copy(
                src_ref=recv.at[c, pl.ds(peer * 2, 2)],
                dst_ref=out.at[:, there],
                send_sem=out_s.at[c],
                recv_sem=out_r,
                device_id=(peer, gy),
                device_id_type=MESH,
            ).start()
            return carry2

        lax.fori_loop(1, nx, one, 0)
        pltpu.make_async_copy(
            recv.at[c, pl.ds(gx * 2, 2)], out.at[:, there], out_l.at[c]
        ).start()
        return carry

    lax.fori_loop(0, chunks, work, 0)

    def finish(c, carry):
        some = recv.at[c, pl.ds(0, 2 * (nx - 1))]
        pltpu.make_async_copy(some, some, in_s.at[c]).wait()
        pltpu.make_async_copy(some, some, out_s.at[c]).wait()
        there = out.at[:, gx * chunks + c]
        pltpu.make_async_copy(recv.at[c, pl.ds(gx * 2, 2)], there, out_l.at[c]).wait()
        return carry

    lax.fori_loop(0, chunks, finish, 0)
    rest = out.at[:, pl.ds(0, (nx - 1) * chunks)]
    pltpu.make_async_copy(rest, rest, out_r).wait()


def local(nx, ny, ensemble, obs_values, obs_error, tile_weight, owner_device, obs_cells):
    own, length, cols = ensemble.shape
    nb, nobs = obs_cells.shape
    members = own * nx
    rows = length // nx
    chunks = rows // CH
    dims = (nx, ny, members, rows, cols, nb, nobs)
    hbm = pl.BlockSpec(memory_space=pltpu.HBM)
    dma = pltpu.SemaphoreType.DMA
    tiles = ensemble.reshape(own, length // CH, CH, cols // 128, 128).transpose(0, 1, 3, 2, 4)
    result = pl.pallas_call(
        functools.partial(kernel, dims),
        out_shape=pltpu.VMEM(tiles.shape, F32),
        in_specs=[hbm] * 6,
        out_specs=pl.BlockSpec(memory_space=pl.ANY),
        scratch_shapes=[
            pltpu.SMEM((nb,), jnp.int32),
            pltpu.SMEM((nb, nobs), jnp.int32),
            pltpu.VMEM((nb, nobs), jnp.int32),
            pltpu.VMEM((nb, nobs), F32),
            pltpu.VMEM((nb, nobs), F32),
            pltpu.VMEM((nb, nobs), F32),
            pltpu.VMEM(tiles.shape, F32),
            pltpu.VMEM((chunks, members, cols // 128, CH, 128), F32),
            pltpu.VMEM((2, nb * nobs, 128), F32),
            pltpu.VMEM((16, nobs), F32),
            pltpu.VMEM((2 * ny, nobs), F32),
            pltpu.VMEM((ny, 2 * nx, nobs), F32),
            pltpu.VMEM((members, nb * nobs), F32),
            pltpu.VMEM((nb, nobs, 4 * members), BF16),
            pltpu.VMEM((nb, 2 * members, 2 * nobs), BF16),
            pltpu.VMEM((nb, nobs, cols), F32),
            pltpu.VMEM((nb, nobs, 128), F32),
            dma,
            dma,
            dma,
            dma,
            dma,
            dma,
            dma((chunks,)),
            dma((chunks,)),
            dma((chunks,)),
            dma((chunks,)),
            dma,
            dma((chunks,)),
            dma((7,)),
        ],
        compiler_params=pltpu.CompilerParams(
            collective_id=0, has_side_effects=True, vmem_limit_bytes=52 * 1024 * 1024
        ),
    )(
        owner_device,
        obs_cells,
        obs_values,
        obs_error,
        tile_weight.reshape(nb, nobs),
        tiles,
    )
    return result.transpose(0, 1, 3, 2, 4).reshape(ensemble.shape)


def solution(mesh):
    placed = (P("gx", None, "gy"), P(), P(), P(None, None, "gx", "gy"), P(), P())
    return jax.shard_map(
        functools.partial(local, mesh.shape["gx"], mesh.shape["gy"]),
        mesh=mesh,
        in_specs=placed,
        out_specs=P("gx", None, "gy"),
        check_vma=False,
    )
```

```python
import functools

import jax
import jax.numpy as jnp
from jax import lax
from jax.experimental import pallas as pl
from jax.experimental.pallas import tpu as pltpu
from jax.sharding import PartitionSpec as P

MESH = pl.DeviceIdType.MESH
EPSILON = 1e-06
F32 = jnp.float32
BF16 = jnp.bfloat16
HI = lax.Precision.HIGHEST
CH = 8
GROUP = 4
EARLY = 2
MIDDLE = 3
LATE = 4
PAIRS = ((0, 1), (0, 2), (0, 3), (1, 2), (1, 3), (2, 3))


def split(a):
    hi = a.astype(BF16)
    return hi, (a - hi.astype(F32)).astype(BF16)


def kernel(
    dims,
    owner_h,
    cells_h,
    values_h,
    errors_h,
    weight_h,
    ens_h,
    out,
    owner_s,
    cells_s,
    cells_v,
    values_v,
    errors_v,
    weight_v,
    ens,
    recv,
    stage,
    pay,
    gyb,
    gxb,
    xobs,
    a_tab,
    i_tab,
    t_tab,
    o_tab,
    gy_s,
    gy_r,
    gx_s,
    gx_r,
    all_s,
    all_r,
    in_s,
    in_r,
    in_l,
    out_s,
    out_r,
    out_l,
    load,
    gate_sem,
    open_sem,
):
    nx, ny, members, rows, cols, nb, nobs = dims
    chunks = rows // CH
    sides = cols // 128
    reach = float(rows * nx // 4)
    gx = lax.axis_index("gx")
    gy = lax.axis_index("gy")
    px = gx // 8
    pz = lax.rem(gx, 8)

    def partner(q):
        t = q // 4
        hop = (t + 1) // 2
        dz = jnp.where(lax.rem(t, 2) == 1, hop, 8 - hop)
        return lax.rem(px + lax.rem(q, 4), 4) * 8 + lax.rem(pz + dz, 8)

    barrier = pltpu.get_barrier_semaphore()

    def greet_x(q, c):
        pl.semaphore_signal(
            barrier, inc=1, device_id=(lax.rem(gx + q, nx), gy), device_id_type=MESH
        )
        return c

    def greet_y(q, c):
        pl.semaphore_signal(
            barrier, inc=1, device_id=(gx, lax.rem(gy + q, ny)), device_id_type=MESH
        )
        return c

    gate = nx - 1
    lax.fori_loop(1, nx, greet_x, 0)

    @pl.when(gx == gate)
    def _():
        lax.fori_loop(1, ny, greet_y, 0)

    loads = [
        pltpu.make_async_copy(src, dst, load.at[n])
        for n, (src, dst) in enumerate(
            (
                (owner_h, owner_s),
                (cells_h, cells_s),
                (cells_h, cells_v),
                (values_h, values_v),
                (errors_h, errors_v),
                (weight_h, weight_v),
                (ens_h, ens),
            )
        )
    ]
    for copy in loads:
        copy.start()

    def send_in(c, carry):
        def one(q, carry2):
            peer = partner(q)
            pltpu.make_async_remote_copy(
                src_ref=ens_h.at[:, peer * chunks + c],
                dst_ref=recv.at[c, pl.ds(gx * 2, 2)],
                send_sem=in_s.at[c],
                recv_sem=in_r.at[c],
                device_id=(peer, gy),
                device_id_type=MESH,
            ).start()
            return carry2

        lax.fori_loop(1, nx, one, 0)
        pltpu.make_async_copy(
            ens_h.at[:, gx * chunks + c], recv.at[c, pl.ds(gx * 2, 2)], in_l.at[c]
        ).start()
        return carry

    def plane_ready(q, c):
        pl.semaphore_signal(
            gate_sem, inc=1, device_id=(gx, lax.rem(gy + q, ny)), device_id_type=MESH
        )
        return c

    def all_ready(q, c):
        pl.semaphore_signal(
            open_sem, inc=1, device_id=(lax.rem(gx + q, nx), gy), device_id_type=MESH
        )
        return c

    @pl.when(gx != gate)
    def _():
        pl.semaphore_wait(barrier, nx - 1)

    @pl.when(gx == gate)
    def _():
        pl.semaphore_wait(barrier, nx + ny - 2)
        lax.fori_loop(1, ny, plane_ready, 0)

    lax.fori_loop(0, EARLY, send_in, 0)

    @pl.when(gx == gate)
    def _():
        pl.semaphore_wait(gate_sem, ny - 1)
        lax.fori_loop(1, nx, all_ready, 0)

    for copy in loads:
        copy.wait()

    lane = lax.broadcasted_iota(jnp.int32, (nobs, 128), 1)
    cells = cells_v[...]
    cx = cells // cols
    cy = cells - cx * cols
    ox_rows, oy_rows = [], []
    for b in range(nb):
        io = owner_s[b] // ny
        jo = owner_s[b] - io * ny
        ox_rows.append((cx[b : b + 1] + io * rows).astype(F32) * (1.0 / reach))
        oy_rows.append((cy[b : b + 1] + jo * cols).astype(F32) * (1.0 / reach))
    table = jnp.concatenate(
        ox_rows + oy_rows + [(cy - cy // 128 * 128).astype(F32), jnp.zeros((nobs - 3 * nb, nobs), F32)], axis=0
    )
    table_t = table.T

    lane_pos = lane.astype(F32)
    for b in range(nb):
        base = (owner_s[b] // ny) * rows

        def fetch(k, c, b=b, base=base):
            cell = cells_s[b, k]
            row = base + cell // cols
            side = lax.rem(cell, cols) // 128
            for m in range(2):
                stage[m, pl.ds(b * nobs + k, 1), :] = ens[
                    m, row // CH, side, pl.ds(lax.rem(row, CH), 1), :
                ]
            return c

        lax.fori_loop(0, nobs, fetch, 0, unroll=8)
    picked = jnp.zeros((nobs, 128), F32)
    for b in range(nb):
        hit = lane_pos == table_t[:, 2 * nb + b : 2 * nb + b + 1]
        mine = (owner_s[b] - (owner_s[b] // ny) * ny == gy).astype(F32)
        for m in range(2):
            rows_here = stage[m, b * nobs : (b + 1) * nobs, :]
            col = jnp.sum(jnp.where(hit, rows_here, 0.0), axis=1, keepdims=True) * mine
            picked = jnp.where(lane == 2 * b + m, col, picked)
    packet = picked.T[:16]
    line = lax.broadcasted_iota(jnp.int32, (16, nobs), 0)
    for n, (b, later) in enumerate(PAIRS):
        mine = (owner_s[later] == gx * ny + gy).astype(F32)
        packet = jnp.where(line == 2 * nb + n, weight_v[b : b + 1, :] * mine, packet)
    pay[...] = packet
    for i in range(2):
        gyb[pl.ds(2 * gy + i, 1), :] = pay[pl.ds(2 * gy + i, 1), :]

    @pl.when(gx != gate)
    def _():
        pl.semaphore_wait(open_sem, 1)

    def send_y(q, c):
        peer = lax.rem(gy + q, ny)
        pltpu.make_async_remote_copy(
            src_ref=pay.at[pl.ds(2 * peer, 2), :],
            dst_ref=gyb.at[pl.ds(2 * gy, 2), :],
            send_sem=gy_s,
            recv_sem=gy_r,
            device_id=(gx, peer),
            device_id_type=MESH,
        ).start()
        return c

    lax.fori_loop(1, ny, send_y, 0)
    lax.fori_loop(EARLY, MIDDLE, send_in, 0)

    part = gyb.at[pl.ds(0, 2 * (ny - 1)), :]
    pltpu.make_async_copy(part, part, gy_r).wait()
    pltpu.make_async_copy(part, part, gy_s).wait()
    for i in range(2):
        gxb[gy, pl.ds(2 * gx + i, 1), :] = jnp.sum(
            gyb[pl.ds(i, ny, stride=2), :], axis=0, keepdims=True
        )

    def send_x(q, c):
        mine = gxb.at[gy, pl.ds(2 * gx, 2), :]
        pltpu.make_async_remote_copy(
            src_ref=mine,
            dst_ref=mine,
            send_sem=gx_s,
            recv_sem=gx_r,
            device_id=(partner(q), gy),
            device_id_type=MESH,
        ).start()
        return c

    lax.fori_loop(1, nx, send_x, 0)
    lax.fori_loop(MIDDLE, LATE, send_in, 0)
    part = gxb.at[0, pl.ds(0, 2 * (nx - 1)), :]
    pltpu.make_async_copy(part, part, gx_r).wait()
    pltpu.make_async_copy(part, part, gx_s).wait()

    def send_all(q, c):
        pltpu.make_async_remote_copy(
            src_ref=gxb.at[gy],
            dst_ref=gxb.at[gy],
            send_sem=all_s,
            recv_sem=all_r,
            device_id=(gx, lax.rem(gy + q, ny)),
            device_id_type=MESH,
        ).start()
        return c

    lax.fori_loop(1, ny, send_all, 0)
    lax.fori_loop(LATE, chunks, send_in, 0)
    part = gxb.at[pl.ds(0, ny - 1)]
    pltpu.make_async_copy(part, part, all_r).wait()
    pltpu.make_async_copy(part, part, all_s).wait()

    for b in range(nb):
        xobs[:, b * nobs : (b + 1) * nobs] = gxb[b]
    w_rows = [
        jnp.sum(gxb[nb + n // 2, pl.ds(n % 2, nx, stride=2), :], axis=0, keepdims=True)
        for n in range(len(PAIRS))
    ]
    w_t = jnp.concatenate(w_rows + [jnp.zeros((nobs - len(PAIRS), nobs), F32)], axis=0).T

    y_here = (
        lax.broadcasted_iota(jnp.int32, (nobs, cols), 1) + gy * cols
    ).astype(F32) * (1.0 / reach)
    for b in range(nb):
        prior = xobs[:, b * nobs : (b + 1) * nobs]
        average = jnp.mean(prior, axis=0, keepdims=True)
        anomaly = prior - average
        spread = jnp.sum(anomaly * anomaly, axis=0, keepdims=True) / (members - 1) + EPSILON
        noise = errors_v[b : b + 1, :]
        post_var = 1.0 / (1.0 / spread + 1.0 / noise)
        post_mean = post_var * (average / spread + values_v[b : b + 1, :] / noise)
        increment = post_mean - average + (jnp.sqrt(post_var / spread) - 1.0) * anomaly
        scaled = anomaly * (1.0 / ((members - 1) * spread))
        ox = table_t[:, b : b + 1]
        oy = table_t[:, nb + b : nb + b + 1]
        if b < nb - 1:
            later = xobs[:, (b + 1) * nobs :]
            deviation = later - jnp.mean(later, axis=0, keepdims=True)
            cov = jnp.dot(scaled.T, deviation, precision=HI, preferred_element_type=F32)
            gains = []
            for later_b in range(b + 1, nb):
                dx = table[later_b : later_b + 1] - ox
                dy = table[nb + later_b : nb + later_b + 1] - oy
                n = PAIRS.index((b, later_b))
                taper = w_t[:, n : n + 1] / (1.0 + (dx * dx + dy * dy))
                at = (later_b - b - 1) * nobs
                gains.append(cov[:, at : at + nobs] * taper)
            gain = jnp.concatenate(gains, axis=1)
            xobs[:, (b + 1) * nobs :] = later + jnp.dot(
                increment, gain, precision=HI, preferred_element_type=F32
            )
        a_hi, a_lo = split((scaled * weight_v[b : b + 1, :]).T)
        a_tab[b] = jnp.concatenate([a_hi, a_lo, a_hi, a_lo], axis=1)
        i_hi, i_lo = split(increment)
        i_tab[b] = jnp.concatenate(
            [jnp.concatenate([i_hi, i_hi], axis=1), jnp.concatenate([i_lo, i_lo], axis=1)],
            axis=0,
        )
        dy = y_here - oy
        t_tab[b] = 1.0 + dy * dy
        o_tab[b] = jnp.broadcast_to(ox, (nobs, 128))

    def work(c, carry):
        some = recv.at[c, pl.ds(0, 2 * (nx - 1))]
        pltpu.make_async_copy(some, some, in_r.at[c]).wait()
        own = recv.at[c, pl.ds(gx * 2, 2)]
        pltpu.make_async_copy(own, own, in_l.at[c]).wait()
        flat = recv.at[c].reshape(members * sides * CH, 128)

        def group(g, carry2):
            first = g * GROUP
            x = jnp.concatenate(
                [
                    flat[pl.ds(first + r + h * CH, members, stride=sides * CH), :]
                    for r in range(GROUP)
                    for h in range(sides)
                ],
                axis=1,
            )
            for b in range(nb):
                deviation = x - jnp.mean(x, axis=0, keepdims=True)
                d_hi, d_lo = split(deviation)
                cov = jnp.dot(
                    a_tab[b],
                    jnp.concatenate([d_hi, d_hi, d_lo, d_lo], axis=0),
                    preferred_element_type=F32,
                )
                gains = []
                for r in range(GROUP):
                    x_here = (gx * rows + c * CH + first + r).astype(F32) * (1.0 / reach)
                    dx = x_here - o_tab[b]
                    dx = dx * dx
                    far = t_tab[b] + jnp.concatenate([dx] * sides, axis=1)
                    gains.append(cov[:, r * cols : (r + 1) * cols] / far)
                g_hi, g_lo = split(jnp.concatenate(gains, axis=1))
                change = jnp.dot(
                    i_tab[b],
                    jnp.concatenate([g_hi, g_lo], axis=0),
                    preferred_element_type=F32,
                )
                x = x + (change[:members] + change[members:])
            for r in range(GROUP):
                for h in range(sides):
                    at = r * cols + h * 128
                    flat[pl.ds(first + r + h * CH, members, stride=sides * CH), :] = x[
                        :, at : at + 128
                    ]
            return carry2

        lax.fori_loop(0, CH // GROUP, group, 0)

        there = gx * chunks + c

        def one(q, carry2):
            peer = partner(q)
            pltpu.make_async_remote_copy(
                src_ref=recv.at[c, pl.ds(peer * 2, 2)],
                dst_ref=out.at[:, there],
                send_sem=out_s.at[c],
                recv_sem=out_r,
                device_id=(peer, gy),
                device_id_type=MESH,
            ).start()
            return carry2

        lax.fori_loop(1, nx, one, 0)
        pltpu.make_async_copy(
            recv.at[c, pl.ds(gx * 2, 2)], out.at[:, there], out_l.at[c]
        ).start()
        return carry

    lax.fori_loop(0, chunks, work, 0)

    def finish(c, carry):
        some = recv.at[c, pl.ds(0, 2 * (nx - 1))]
        pltpu.make_async_copy(some, some, in_s.at[c]).wait()
        pltpu.make_async_copy(some, some, out_s.at[c]).wait()
        there = out.at[:, gx * chunks + c]
        pltpu.make_async_copy(recv.at[c, pl.ds(gx * 2, 2)], there, out_l.at[c]).wait()
        return carry

    lax.fori_loop(0, chunks, finish, 0)
    rest = out.at[:, pl.ds(0, (nx - 1) * chunks)]
    pltpu.make_async_copy(rest, rest, out_r).wait()


def local(nx, ny, ensemble, obs_values, obs_error, tile_weight, owner_device, obs_cells):
    own, length, cols = ensemble.shape
    nb, nobs = obs_cells.shape
    members = own * nx
    rows = length // nx
    chunks = rows // CH
    dims = (nx, ny, members, rows, cols, nb, nobs)
    hbm = pl.BlockSpec(memory_space=pltpu.HBM)
    dma = pltpu.SemaphoreType.DMA
    tiles = ensemble.reshape(own, length // CH, CH, cols // 128, 128).transpose(0, 1, 3, 2, 4)
    result = pl.pallas_call(
        functools.partial(kernel, dims),
        out_shape=pltpu.VMEM(tiles.shape, F32),
        in_specs=[hbm] * 6,
        out_specs=pl.BlockSpec(memory_space=pl.ANY),
        scratch_shapes=[
            pltpu.SMEM((nb,), jnp.int32),
            pltpu.SMEM((nb, nobs), jnp.int32),
            pltpu.VMEM((nb, nobs), jnp.int32),
            pltpu.VMEM((nb, nobs), F32),
            pltpu.VMEM((nb, nobs), F32),
            pltpu.VMEM((nb, nobs), F32),
            pltpu.VMEM(tiles.shape, F32),
            pltpu.VMEM((chunks, members, cols // 128, CH, 128), F32),
            pltpu.VMEM((2, nb * nobs, 128), F32),
            pltpu.VMEM((16, nobs), F32),
            pltpu.VMEM((2 * ny, nobs), F32),
            pltpu.VMEM((ny, 2 * nx, nobs), F32),
            pltpu.VMEM((members, nb * nobs), F32),
            pltpu.VMEM((nb, nobs, 4 * members), BF16),
            pltpu.VMEM((nb, 2 * members, 2 * nobs), BF16),
            pltpu.VMEM((nb, nobs, cols), F32),
            pltpu.VMEM((nb, nobs, 128), F32),
            dma,
            dma,
            dma,
            dma,
            dma,
            dma,
            dma((chunks,)),
            dma((chunks,)),
            dma((chunks,)),
            dma((chunks,)),
            dma,
            dma((chunks,)),
            dma((7,)),
            pltpu.SemaphoreType.REGULAR,
            pltpu.SemaphoreType.REGULAR,
        ],
        compiler_params=pltpu.CompilerParams(
            collective_id=0, has_side_effects=True, vmem_limit_bytes=52 * 1024 * 1024
        ),
    )(
        owner_device,
        obs_cells,
        obs_values,
        obs_error,
        tile_weight.reshape(nb, nobs),
        tiles,
    )
    return result.transpose(0, 1, 3, 2, 4).reshape(ensemble.shape)


def solution(mesh):
    placed = (P("gx", None, "gy"), P(), P(), P(None, None, "gx", "gy"), P(), P())
    return jax.shard_map(
        functools.partial(local, mesh.shape["gx"], mesh.shape["gy"]),
        mesh=mesh,
        in_specs=placed,
        out_specs=P("gx", None, "gy"),
        check_vma=False,
    )
```

```python
import functools

import jax
import jax.numpy as jnp
from jax import lax
from jax.experimental import pallas as pl
from jax.experimental.pallas import tpu as pltpu
from jax.sharding import PartitionSpec as P

MESH = pl.DeviceIdType.MESH
EPSILON = 1e-06
F32 = jnp.float32
BF16 = jnp.bfloat16
HI = lax.Precision.HIGHEST
CH = 8
GROUP = 4
EARLY = 2
MIDDLE = 3
LATE = 4
LAST = 2
PAIRS = ((0, 1), (0, 2), (0, 3), (1, 2), (1, 3), (2, 3))


def split(a):
    hi = a.astype(BF16)
    return hi, (a - hi.astype(F32)).astype(BF16)


def kernel(
    dims,
    owner_h,
    cells_h,
    values_h,
    errors_h,
    weight_h,
    ens_h,
    out,
    owner_s,
    cells_s,
    cells_v,
    values_v,
    errors_v,
    weight_v,
    ens,
    recv,
    stage,
    pay,
    gyb,
    gxb,
    xobs,
    a_tab,
    i_tab,
    t_tab,
    o_tab,
    gy_s,
    gy_r,
    gx_s,
    gx_r,
    all_s,
    all_r,
    in_s,
    in_r,
    in_l,
    out_s,
    out_r,
    out_l,
    load,
    gate_sem,
    open_sem,
):
    nx, ny, members, rows, cols, nb, nobs = dims
    chunks = rows // CH
    sides = cols // 128
    reach = float(rows * nx // 4)
    gx = lax.axis_index("gx")
    gy = lax.axis_index("gy")
    px = gx // 8
    pz = lax.rem(gx, 8)

    def partner(q):
        t = q // 4
        hop = (t + 1) // 2
        dz = jnp.where(lax.rem(t, 2) == 1, hop, 8 - hop)
        return lax.rem(px + lax.rem(q, 4), 4) * 8 + lax.rem(pz + dz, 8)

    barrier = pltpu.get_barrier_semaphore()

    def greet_x(q, c):
        pl.semaphore_signal(
            barrier, inc=1, device_id=(lax.rem(gx + q, nx), gy), device_id_type=MESH
        )
        return c

    def greet_y(q, c):
        pl.semaphore_signal(
            barrier, inc=1, device_id=(gx, lax.rem(gy + q, ny)), device_id_type=MESH
        )
        return c

    gate = nx - 1
    lax.fori_loop(1, nx, greet_x, 0)

    @pl.when(gx == gate)
    def _():
        lax.fori_loop(1, ny, greet_y, 0)

    loads = [
        pltpu.make_async_copy(src, dst, load.at[n])
        for n, (src, dst) in enumerate(
            (
                (owner_h, owner_s),
                (cells_h, cells_s),
                (cells_h, cells_v),
                (values_h, values_v),
                (errors_h, errors_v),
                (weight_h, weight_v),
                (ens_h, ens),
            )
        )
    ]
    for copy in loads:
        copy.start()

    def send_in(c, carry):
        def one(q, carry2):
            peer = partner(q)
            pltpu.make_async_remote_copy(
                src_ref=ens_h.at[:, peer * chunks + c],
                dst_ref=recv.at[c, pl.ds(gx * 2, 2)],
                send_sem=in_s.at[c],
                recv_sem=in_r.at[c],
                device_id=(peer, gy),
                device_id_type=MESH,
            ).start()
            return carry2

        lax.fori_loop(1, nx, one, 0)
        pltpu.make_async_copy(
            ens_h.at[:, gx * chunks + c], recv.at[c, pl.ds(gx * 2, 2)], in_l.at[c]
        ).start()
        return carry

    def plane_ready(q, c):
        pl.semaphore_signal(
            gate_sem, inc=1, device_id=(gx, lax.rem(gy + q, ny)), device_id_type=MESH
        )
        return c

    def all_ready(q, c):
        pl.semaphore_signal(
            open_sem, inc=1, device_id=(lax.rem(gx + q, nx), gy), device_id_type=MESH
        )
        return c

    @pl.when(gx != gate)
    def _():
        pl.semaphore_wait(barrier, nx - 1)

    @pl.when(gx == gate)
    def _():
        pl.semaphore_wait(barrier, nx + ny - 2)
        lax.fori_loop(1, ny, plane_ready, 0)

    lax.fori_loop(0, EARLY, send_in, 0)

    @pl.when(gx == gate)
    def _():
        pl.semaphore_wait(gate_sem, ny - 1)
        lax.fori_loop(1, nx, all_ready, 0)

    for copy in loads:
        copy.wait()

    lane = lax.broadcasted_iota(jnp.int32, (nobs, 128), 1)
    cells = cells_v[...]
    cx = cells // cols
    cy = cells - cx * cols
    ox_rows, oy_rows = [], []
    for b in range(nb):
        io = owner_s[b] // ny
        jo = owner_s[b] - io * ny
        ox_rows.append((cx[b : b + 1] + io * rows).astype(F32) * (1.0 / reach))
        oy_rows.append((cy[b : b + 1] + jo * cols).astype(F32) * (1.0 / reach))
    table = jnp.concatenate(
        ox_rows + oy_rows + [(cy - cy // 128 * 128).astype(F32), jnp.zeros((nobs - 3 * nb, nobs), F32)], axis=0
    )
    table_t = table.T

    lane_pos = lane.astype(F32)
    for b in range(nb):
        base = (owner_s[b] // ny) * rows

        def fetch(k, c, b=b, base=base):
            cell = cells_s[b, k]
            row = base + cell // cols
            side = lax.rem(cell, cols) // 128
            for m in range(2):
                stage[m, pl.ds(b * nobs + k, 1), :] = ens[
                    m, row // CH, side, pl.ds(lax.rem(row, CH), 1), :
                ]
            return c

        lax.fori_loop(0, nobs, fetch, 0, unroll=8)
    picked = jnp.zeros((nobs, 128), F32)
    for b in range(nb):
        hit = lane_pos == table_t[:, 2 * nb + b : 2 * nb + b + 1]
        mine = (owner_s[b] - (owner_s[b] // ny) * ny == gy).astype(F32)
        for m in range(2):
            rows_here = stage[m, b * nobs : (b + 1) * nobs, :]
            col = jnp.sum(jnp.where(hit, rows_here, 0.0), axis=1, keepdims=True) * mine
            picked = jnp.where(lane == 2 * b + m, col, picked)
    packet = picked.T[:16]
    line = lax.broadcasted_iota(jnp.int32, (16, nobs), 0)
    for n, (b, later) in enumerate(PAIRS):
        mine = (owner_s[later] == gx * ny + gy).astype(F32)
        packet = jnp.where(line == 2 * nb + n, weight_v[b : b + 1, :] * mine, packet)
    pay[...] = packet
    for i in range(2):
        gyb[pl.ds(2 * gy + i, 1), :] = pay[pl.ds(2 * gy + i, 1), :]

    @pl.when(gx != gate)
    def _():
        pl.semaphore_wait(open_sem, 1)

    def send_y(q, c):
        peer = lax.rem(gy + q, ny)
        pltpu.make_async_remote_copy(
            src_ref=pay.at[pl.ds(2 * peer, 2), :],
            dst_ref=gyb.at[pl.ds(2 * gy, 2), :],
            send_sem=gy_s,
            recv_sem=gy_r,
            device_id=(gx, peer),
            device_id_type=MESH,
        ).start()
        return c

    lax.fori_loop(1, ny, send_y, 0)
    lax.fori_loop(EARLY, MIDDLE, send_in, 0)

    part = gyb.at[pl.ds(0, 2 * (ny - 1)), :]
    pltpu.make_async_copy(part, part, gy_r).wait()
    pltpu.make_async_copy(part, part, gy_s).wait()
    for i in range(2):
        gxb[gy, pl.ds(2 * gx + i, 1), :] = jnp.sum(
            gyb[pl.ds(i, ny, stride=2), :], axis=0, keepdims=True
        )

    def send_x(q, c):
        mine = gxb.at[gy, pl.ds(2 * gx, 2), :]
        pltpu.make_async_remote_copy(
            src_ref=mine,
            dst_ref=mine,
            send_sem=gx_s,
            recv_sem=gx_r,
            device_id=(partner(q), gy),
            device_id_type=MESH,
        ).start()
        return c

    lax.fori_loop(1, nx, send_x, 0)
    lax.fori_loop(MIDDLE, LATE, send_in, 0)
    part = gxb.at[0, pl.ds(0, 2 * (nx - 1)), :]
    pltpu.make_async_copy(part, part, gx_r).wait()
    pltpu.make_async_copy(part, part, gx_s).wait()

    def send_all(q, c):
        pltpu.make_async_remote_copy(
            src_ref=gxb.at[gy],
            dst_ref=gxb.at[gy],
            send_sem=all_s,
            recv_sem=all_r,
            device_id=(gx, lax.rem(gy + q, ny)),
            device_id_type=MESH,
        ).start()
        return c

    lax.fori_loop(1, ny, send_all, 0)
    lax.fori_loop(LATE, chunks, send_in, 0)
    part = gxb.at[pl.ds(0, ny - 1)]
    pltpu.make_async_copy(part, part, all_r).wait()
    pltpu.make_async_copy(part, part, all_s).wait()

    for b in range(nb):
        xobs[:, b * nobs : (b + 1) * nobs] = gxb[b]
    w_rows = [
        jnp.sum(gxb[nb + n // 2, pl.ds(n % 2, nx, stride=2), :], axis=0, keepdims=True)
        for n in range(len(PAIRS))
    ]
    w_t = jnp.concatenate(w_rows + [jnp.zeros((nobs - len(PAIRS), nobs), F32)], axis=0).T

    y_here = (
        lax.broadcasted_iota(jnp.int32, (nobs, cols), 1) + gy * cols
    ).astype(F32) * (1.0 / reach)
    for b in range(nb):
        prior = xobs[:, b * nobs : (b + 1) * nobs]
        average = jnp.mean(prior, axis=0, keepdims=True)
        anomaly = prior - average
        spread = jnp.sum(anomaly * anomaly, axis=0, keepdims=True) / (members - 1) + EPSILON
        noise = errors_v[b : b + 1, :]
        post_var = 1.0 / (1.0 / spread + 1.0 / noise)
        post_mean = post_var * (average / spread + values_v[b : b + 1, :] / noise)
        increment = post_mean - average + (jnp.sqrt(post_var / spread) - 1.0) * anomaly
        scaled = anomaly * (1.0 / ((members - 1) * spread))
        ox = table_t[:, b : b + 1]
        oy = table_t[:, nb + b : nb + b + 1]
        if b < nb - 1:
            later = xobs[:, (b + 1) * nobs :]
            deviation = later - jnp.mean(later, axis=0, keepdims=True)
            cov = jnp.dot(scaled.T, deviation, precision=HI, preferred_element_type=F32)
            gains = []
            for later_b in range(b + 1, nb):
                dx = table[later_b : later_b + 1] - ox
                dy = table[nb + later_b : nb + later_b + 1] - oy
                n = PAIRS.index((b, later_b))
                taper = w_t[:, n : n + 1] / (1.0 + (dx * dx + dy * dy))
                at = (later_b - b - 1) * nobs
                gains.append(cov[:, at : at + nobs] * taper)
            gain = jnp.concatenate(gains, axis=1)
            xobs[:, (b + 1) * nobs :] = later + jnp.dot(
                increment, gain, precision=HI, preferred_element_type=F32
            )
        a_hi, a_lo = split((scaled * weight_v[b : b + 1, :]).T)
        a_tab[b] = jnp.concatenate([a_hi, a_lo, a_hi, a_lo], axis=1)
        i_hi, i_lo = split(increment)
        i_tab[b] = jnp.concatenate(
            [jnp.concatenate([i_hi, i_hi], axis=1), jnp.concatenate([i_lo, i_lo], axis=1)],
            axis=0,
        )
        dy = y_here - oy
        t_tab[b] = 1.0 + dy * dy
        o_tab[b] = jnp.broadcast_to(ox, (nobs, 128))

    def work(c, carry):
        some = recv.at[c, pl.ds(0, 2 * (nx - 1))]
        pltpu.make_async_copy(some, some, in_r.at[c]).wait()
        own = recv.at[c, pl.ds(gx * 2, 2)]
        pltpu.make_async_copy(own, own, in_l.at[c]).wait()
        flat = recv.at[c].reshape(members * sides * CH, 128)

        def group(g, carry2):
            first = g * GROUP
            x = jnp.concatenate(
                [
                    flat[pl.ds(first + r + h * CH, members, stride=sides * CH), :]
                    for r in range(GROUP)
                    for h in range(sides)
                ],
                axis=1,
            )
            for b in range(nb):
                deviation = x - jnp.mean(x, axis=0, keepdims=True)
                d_hi, d_lo = split(deviation)
                cov = jnp.dot(
                    a_tab[b],
                    jnp.concatenate([d_hi, d_hi, d_lo, d_lo], axis=0),
                    preferred_element_type=F32,
                )
                gains = []
                for r in range(GROUP):
                    x_here = (gx * rows + c * CH + first + r).astype(F32) * (1.0 / reach)
                    dx = x_here - o_tab[b]
                    dx = dx * dx
                    far = t_tab[b] + jnp.concatenate([dx] * sides, axis=1)
                    gains.append(cov[:, r * cols : (r + 1) * cols] / far)
                g_hi, g_lo = split(jnp.concatenate(gains, axis=1))
                change = jnp.dot(
                    i_tab[b],
                    jnp.concatenate([g_hi, g_lo], axis=0),
                    preferred_element_type=F32,
                )
                x = x + (change[:members] + change[members:])
            for r in range(GROUP):
                for h in range(sides):
                    at = r * cols + h * 128
                    flat[pl.ds(first + r + h * CH, members, stride=sides * CH), :] = x[
                        :, at : at + 128
                    ]
            return carry2

        lax.fori_loop(0, CH // GROUP, group, 0)

        there = gx * chunks + c

        def send_out(peer):
            pltpu.make_async_remote_copy(
                src_ref=recv.at[c, pl.ds(peer * 2, 2)],
                dst_ref=out.at[:, there],
                send_sem=out_s.at[c],
                recv_sem=out_r,
                device_id=(peer, gy),
                device_id_type=MESH,
            ).start()

        def one(q, carry2):
            t = q // 4
            z_there = t // 4 * 4 + lax.rem(t + pz, 4)
            by_half = lax.rem(px + lax.rem(q, 4), 4) * 8 + z_there
            peer = jnp.where(c < chunks - LAST, partner(q), by_half)

            @pl.when(peer != gx)
            def _():
                send_out(peer)

            return carry2

        lax.fori_loop(0, nx, one, 0)
        pltpu.make_async_copy(
            recv.at[c, pl.ds(gx * 2, 2)], out.at[:, there], out_l.at[c]
        ).start()
        return carry

    lax.fori_loop(0, chunks, work, 0)

    def finish(c, carry):
        some = recv.at[c, pl.ds(0, 2 * (nx - 1))]
        pltpu.make_async_copy(some, some, in_s.at[c]).wait()
        pltpu.make_async_copy(some, some, out_s.at[c]).wait()
        there = out.at[:, gx * chunks + c]
        pltpu.make_async_copy(recv.at[c, pl.ds(gx * 2, 2)], there, out_l.at[c]).wait()
        return carry

    lax.fori_loop(0, chunks, finish, 0)
    rest = out.at[:, pl.ds(0, (nx - 1) * chunks)]
    pltpu.make_async_copy(rest, rest, out_r).wait()


def local(nx, ny, ensemble, obs_values, obs_error, tile_weight, owner_device, obs_cells):
    own, length, cols = ensemble.shape
    nb, nobs = obs_cells.shape
    members = own * nx
    rows = length // nx
    chunks = rows // CH
    dims = (nx, ny, members, rows, cols, nb, nobs)
    hbm = pl.BlockSpec(memory_space=pltpu.HBM)
    dma = pltpu.SemaphoreType.DMA
    tiles = ensemble.reshape(own, length // CH, CH, cols // 128, 128).transpose(0, 1, 3, 2, 4)
    result = pl.pallas_call(
        functools.partial(kernel, dims),
        out_shape=pltpu.VMEM(tiles.shape, F32),
        in_specs=[hbm] * 6,
        out_specs=pl.BlockSpec(memory_space=pl.ANY),
        scratch_shapes=[
            pltpu.SMEM((nb,), jnp.int32),
            pltpu.SMEM((nb, nobs), jnp.int32),
            pltpu.VMEM((nb, nobs), jnp.int32),
            pltpu.VMEM((nb, nobs), F32),
            pltpu.VMEM((nb, nobs), F32),
            pltpu.VMEM((nb, nobs), F32),
            pltpu.VMEM(tiles.shape, F32),
            pltpu.VMEM((chunks, members, cols // 128, CH, 128), F32),
            pltpu.VMEM((2, nb * nobs, 128), F32),
            pltpu.VMEM((16, nobs), F32),
            pltpu.VMEM((2 * ny, nobs), F32),
            pltpu.VMEM((ny, 2 * nx, nobs), F32),
            pltpu.VMEM((members, nb * nobs), F32),
            pltpu.VMEM((nb, nobs, 4 * members), BF16),
            pltpu.VMEM((nb, 2 * members, 2 * nobs), BF16),
            pltpu.VMEM((nb, nobs, cols), F32),
            pltpu.VMEM((nb, nobs, 128), F32),
            dma,
            dma,
            dma,
            dma,
            dma,
            dma,
            dma((chunks,)),
            dma((chunks,)),
            dma((chunks,)),
            dma((chunks,)),
            dma,
            dma((chunks,)),
            dma((7,)),
            pltpu.SemaphoreType.REGULAR,
            pltpu.SemaphoreType.REGULAR,
        ],
        compiler_params=pltpu.CompilerParams(
            collective_id=0, has_side_effects=True, vmem_limit_bytes=52 * 1024 * 1024
        ),
    )(
        owner_device,
        obs_cells,
        obs_values,
        obs_error,
        tile_weight.reshape(nb, nobs),
        tiles,
    )
    return result.transpose(0, 1, 3, 2, 4).reshape(ensemble.shape)


def solution(mesh):
    placed = (P("gx", None, "gy"), P(), P(), P(None, None, "gx", "gy"), P(), P())
    return jax.shard_map(
        functools.partial(local, mesh.shape["gx"], mesh.shape["gy"]),
        mesh=mesh,
        in_specs=placed,
        out_specs=P("gx", None, "gy"),
        check_vma=False,
    )
```

```python
import functools

import jax
import jax.numpy as jnp
from jax import lax
from jax.experimental import pallas as pl
from jax.experimental.pallas import tpu as pltpu
from jax.sharding import PartitionSpec as P

MESH = pl.DeviceIdType.MESH
EPSILON = 1e-06
F32 = jnp.float32
BF16 = jnp.bfloat16
HI = lax.Precision.HIGHEST
CH = 8
GROUP = 4
EARLY = 2
MIDDLE = 3
LATE = 4
PAIRS = ((0, 1), (0, 2), (0, 3), (1, 2), (1, 3), (2, 3))


def split(a):
    hi = a.astype(BF16)
    return hi, (a - hi.astype(F32)).astype(BF16)


def kernel(
    dims,
    owner_h,
    cells_h,
    values_h,
    errors_h,
    weight_h,
    ens_h,
    out,
    owner_s,
    cells_s,
    cells_v,
    values_v,
    errors_v,
    weight_v,
    ens,
    recv,
    stage,
    pay,
    gyb,
    gxb,
    xobs,
    a_tab,
    i_tab,
    t_tab,
    o_tab,
    gy_s,
    gy_r,
    gx_s,
    gx_r,
    all_s,
    all_r,
    in_s,
    in_r,
    in_l,
    out_s,
    out_r,
    out_l,
    load,
    gate_sem,
    open_sem,
):
    nx, ny, members, rows, cols, nb, nobs = dims
    chunks = rows // CH
    sides = cols // 128
    reach = float(rows * nx // 4)
    gx = lax.axis_index("gx")
    gy = lax.axis_index("gy")
    px = gx // 8
    pz = lax.rem(gx, 8)

    def partner(q):
        t = q // 4
        hop = (t + 1) // 2
        dz = jnp.where(lax.rem(t, 2) == 1, hop, 8 - hop)
        return lax.rem(px + lax.rem(q, 4), 4) * 8 + lax.rem(pz + dz, 8)

    barrier = pltpu.get_barrier_semaphore()

    def greet_x(q, c):
        pl.semaphore_signal(
            barrier, inc=1, device_id=(lax.rem(gx + q, nx), gy), device_id_type=MESH
        )
        return c

    def greet_y(q, c):
        pl.semaphore_signal(
            barrier, inc=1, device_id=(gx, lax.rem(gy + q, ny)), device_id_type=MESH
        )
        return c

    gate = nx - 1
    lax.fori_loop(1, nx, greet_x, 0, unroll=True)

    @pl.when(gx == gate)
    def _():
        lax.fori_loop(1, ny, greet_y, 0)

    loads = [
        pltpu.make_async_copy(src, dst, load.at[n])
        for n, (src, dst) in enumerate(
            (
                (owner_h, owner_s),
                (cells_h, cells_s),
                (cells_h, cells_v),
                (values_h, values_v),
                (errors_h, errors_v),
                (weight_h, weight_v),
                (ens_h, ens),
            )
        )
    ]
    for copy in loads:
        copy.start()

    def send_in(c, carry):
        def one(q, carry2):
            peer = partner(q)
            pltpu.make_async_remote_copy(
                src_ref=ens_h.at[:, peer * chunks + c],
                dst_ref=recv.at[c, pl.ds(gx * 2, 2)],
                send_sem=in_s.at[c],
                recv_sem=in_r.at[c],
                device_id=(peer, gy),
                device_id_type=MESH,
            ).start()
            return carry2

        lax.fori_loop(1, nx, one, 0)
        pltpu.make_async_copy(
            ens_h.at[:, gx * chunks + c], recv.at[c, pl.ds(gx * 2, 2)], in_l.at[c]
        ).start()
        return carry

    def plane_ready(q, c):
        pl.semaphore_signal(
            gate_sem, inc=1, device_id=(gx, lax.rem(gy + q, ny)), device_id_type=MESH
        )
        return c

    def all_ready(q, c):
        pl.semaphore_signal(
            open_sem, inc=1, device_id=(lax.rem(gx + q, nx), gy), device_id_type=MESH
        )
        return c

    @pl.when(gx != gate)
    def _():
        pl.semaphore_wait(barrier, nx - 1)

    @pl.when(gx == gate)
    def _():
        pl.semaphore_wait(barrier, nx + ny - 2)
        lax.fori_loop(1, ny, plane_ready, 0)

    lax.fori_loop(0, EARLY, send_in, 0)

    @pl.when(gx == gate)
    def _():
        pl.semaphore_wait(gate_sem, ny - 1)
        lax.fori_loop(1, nx, all_ready, 0)

    for copy in loads:
        copy.wait()

    lane = lax.broadcasted_iota(jnp.int32, (nobs, 128), 1)
    cells = cells_v[...]
    cx = cells // cols
    cy = cells - cx * cols
    ox_rows, oy_rows = [], []
    for b in range(nb):
        io = owner_s[b] // ny
        jo = owner_s[b] - io * ny
        ox_rows.append((cx[b : b + 1] + io * rows).astype(F32) * (1.0 / reach))
        oy_rows.append((cy[b : b + 1] + jo * cols).astype(F32) * (1.0 / reach))
    table = jnp.concatenate(
        ox_rows + oy_rows + [(cy - cy // 128 * 128).astype(F32), jnp.zeros((nobs - 3 * nb, nobs), F32)], axis=0
    )
    table_t = table.T

    lane_pos = lane.astype(F32)
    for b in range(nb):
        base = (owner_s[b] // ny) * rows

        def fetch(k, c, b=b, base=base):
            cell = cells_s[b, k]
            row = base + cell // cols
            side = lax.rem(cell, cols) // 128
            for m in range(2):
                stage[m, pl.ds(b * nobs + k, 1), :] = ens[
                    m, row // CH, side, pl.ds(lax.rem(row, CH), 1), :
                ]
            return c

        lax.fori_loop(0, nobs, fetch, 0, unroll=8)
    picked = jnp.zeros((nobs, 128), F32)
    for b in range(nb):
        hit = lane_pos == table_t[:, 2 * nb + b : 2 * nb + b + 1]
        mine = (owner_s[b] - (owner_s[b] // ny) * ny == gy).astype(F32)
        for m in range(2):
            rows_here = stage[m, b * nobs : (b + 1) * nobs, :]
            col = jnp.sum(jnp.where(hit, rows_here, 0.0), axis=1, keepdims=True) * mine
            picked = jnp.where(lane == 2 * b + m, col, picked)
    packet = picked.T[:16]
    line = lax.broadcasted_iota(jnp.int32, (16, nobs), 0)
    for n, (b, later) in enumerate(PAIRS):
        mine = (owner_s[later] == gx * ny + gy).astype(F32)
        packet = jnp.where(line == 2 * nb + n, weight_v[b : b + 1, :] * mine, packet)
    pay[...] = packet
    for i in range(2):
        gyb[pl.ds(2 * gy + i, 1), :] = pay[pl.ds(2 * gy + i, 1), :]

    @pl.when(gx != gate)
    def _():
        pl.semaphore_wait(open_sem, 1)

    def send_y(q, c):
        peer = lax.rem(gy + q, ny)
        pltpu.make_async_remote_copy(
            src_ref=pay.at[pl.ds(2 * peer, 2), :],
            dst_ref=gyb.at[pl.ds(2 * gy, 2), :],
            send_sem=gy_s,
            recv_sem=gy_r,
            device_id=(gx, peer),
            device_id_type=MESH,
        ).start()
        return c

    lax.fori_loop(1, ny, send_y, 0)
    lax.fori_loop(EARLY, MIDDLE, send_in, 0)

    part = gyb.at[pl.ds(0, 2 * (ny - 1)), :]
    pltpu.make_async_copy(part, part, gy_r).wait()
    pltpu.make_async_copy(part, part, gy_s).wait()
    for i in range(2):
        gxb[gy, pl.ds(2 * gx + i, 1), :] = jnp.sum(
            gyb[pl.ds(i, ny, stride=2), :], axis=0, keepdims=True
        )

    def send_x(q, c):
        mine = gxb.at[gy, pl.ds(2 * gx, 2), :]
        pltpu.make_async_remote_copy(
            src_ref=mine,
            dst_ref=mine,
            send_sem=gx_s,
            recv_sem=gx_r,
            device_id=(partner(q), gy),
            device_id_type=MESH,
        ).start()
        return c

    lax.fori_loop(1, nx, send_x, 0)
    lax.fori_loop(MIDDLE, LATE, send_in, 0)
    part = gxb.at[0, pl.ds(0, 2 * (nx - 1)), :]
    pltpu.make_async_copy(part, part, gx_r).wait()
    pltpu.make_async_copy(part, part, gx_s).wait()

    def send_all(q, c):
        pltpu.make_async_remote_copy(
            src_ref=gxb.at[gy],
            dst_ref=gxb.at[gy],
            send_sem=all_s,
            recv_sem=all_r,
            device_id=(gx, lax.rem(gy + q, ny)),
            device_id_type=MESH,
        ).start()
        return c

    lax.fori_loop(1, ny, send_all, 0)
    lax.fori_loop(LATE, chunks, send_in, 0)
    part = gxb.at[pl.ds(0, ny - 1)]
    pltpu.make_async_copy(part, part, all_r).wait()
    pltpu.make_async_copy(part, part, all_s).wait()

    for b in range(nb):
        xobs[:, b * nobs : (b + 1) * nobs] = gxb[b]
    w_rows = [
        jnp.sum(gxb[nb + n // 2, pl.ds(n % 2, nx, stride=2), :], axis=0, keepdims=True)
        for n in range(len(PAIRS))
    ]
    w_t = jnp.concatenate(w_rows + [jnp.zeros((nobs - len(PAIRS), nobs), F32)], axis=0).T

    y_here = (
        lax.broadcasted_iota(jnp.int32, (nobs, cols), 1) + gy * cols
    ).astype(F32) * (1.0 / reach)
    for b in range(nb):
        prior = xobs[:, b * nobs : (b + 1) * nobs]
        average = jnp.mean(prior, axis=0, keepdims=True)
        anomaly = prior - average
        spread = jnp.sum(anomaly * anomaly, axis=0, keepdims=True) / (members - 1) + EPSILON
        noise = errors_v[b : b + 1, :]
        post_var = 1.0 / (1.0 / spread + 1.0 / noise)
        post_mean = post_var * (average / spread + values_v[b : b + 1, :] / noise)
        increment = post_mean - average + (jnp.sqrt(post_var / spread) - 1.0) * anomaly
        scaled = anomaly * (1.0 / ((members - 1) * spread))
        ox = table_t[:, b : b + 1]
        oy = table_t[:, nb + b : nb + b + 1]
        if b < nb - 1:
            later = xobs[:, (b + 1) * nobs :]
            deviation = later - jnp.mean(later, axis=0, keepdims=True)
            cov = jnp.dot(scaled.T, deviation, precision=HI, preferred_element_type=F32)
            gains = []
            for later_b in range(b + 1, nb):
                dx = table[later_b : later_b + 1] - ox
                dy = table[nb + later_b : nb + later_b + 1] - oy
                n = PAIRS.index((b, later_b))
                taper = w_t[:, n : n + 1] / (1.0 + (dx * dx + dy * dy))
                at = (later_b - b - 1) * nobs
                gains.append(cov[:, at : at + nobs] * taper)
            gain = jnp.concatenate(gains, axis=1)
            xobs[:, (b + 1) * nobs :] = later + jnp.dot(
                increment, gain, precision=HI, preferred_element_type=F32
            )
        a_hi, a_lo = split((scaled * weight_v[b : b + 1, :]).T)
        a_tab[b] = jnp.concatenate([a_hi, a_lo, a_hi, a_lo], axis=1)
        i_hi, i_lo = split(increment)
        i_tab[b] = jnp.concatenate(
            [jnp.concatenate([i_hi, i_hi], axis=1), jnp.concatenate([i_lo, i_lo], axis=1)],
            axis=0,
        )
        dy = y_here - oy
        t_tab[b] = 1.0 + dy * dy
        o_tab[b] = jnp.broadcast_to(ox, (nobs, 128))

    def work(c, carry):
        some = recv.at[c, pl.ds(0, 2 * (nx - 1))]
        pltpu.make_async_copy(some, some, in_r.at[c]).wait()
        own = recv.at[c, pl.ds(gx * 2, 2)]
        pltpu.make_async_copy(own, own, in_l.at[c]).wait()
        flat = recv.at[c].reshape(members * sides * CH, 128)

        def group(g, carry2):
            first = g * GROUP
            x = jnp.concatenate(
                [
                    flat[pl.ds(first + r + h * CH, members, stride=sides * CH), :]
                    for r in range(GROUP)
                    for h in range(sides)
                ],
                axis=1,
            )
            for b in range(nb):
                deviation = x - jnp.mean(x, axis=0, keepdims=True)
                d_hi, d_lo = split(deviation)
                cov = jnp.dot(
                    a_tab[b],
                    jnp.concatenate([d_hi, d_hi, d_lo, d_lo], axis=0),
                    preferred_element_type=F32,
                )
                gains = []
                for r in range(GROUP):
                    x_here = (gx * rows + c * CH + first + r).astype(F32) * (1.0 / reach)
                    dx = x_here - o_tab[b]
                    dx = dx * dx
                    far = t_tab[b] + jnp.concatenate([dx] * sides, axis=1)
                    gains.append(cov[:, r * cols : (r + 1) * cols] / far)
                g_hi, g_lo = split(jnp.concatenate(gains, axis=1))
                change = jnp.dot(
                    i_tab[b],
                    jnp.concatenate([g_hi, g_lo], axis=0),
                    preferred_element_type=F32,
                )
                x = x + (change[:members] + change[members:])
            for r in range(GROUP):
                for h in range(sides):
                    at = r * cols + h * 128
                    flat[pl.ds(first + r + h * CH, members, stride=sides * CH), :] = x[
                        :, at : at + 128
                    ]
            return carry2

        lax.fori_loop(0, CH // GROUP, group, 0)

        there = gx * chunks + c

        def one(q, carry2):
            peer = partner(q)
            pltpu.make_async_remote_copy(
                src_ref=recv.at[c, pl.ds(peer * 2, 2)],
                dst_ref=out.at[:, there],
                send_sem=out_s.at[c],
                recv_sem=out_r,
                device_id=(peer, gy),
                device_id_type=MESH,
            ).start()
            return carry2

        lax.fori_loop(1, nx, one, 0)
        pltpu.make_async_copy(
            recv.at[c, pl.ds(gx * 2, 2)], out.at[:, there], out_l.at[c]
        ).start()
        return carry

    lax.fori_loop(0, chunks, work, 0)

    def finish(c, carry):
        some = recv.at[c, pl.ds(0, 2 * (nx - 1))]
        pltpu.make_async_copy(some, some, in_s.at[c]).wait()
        pltpu.make_async_copy(some, some, out_s.at[c]).wait()
        there = out.at[:, gx * chunks + c]
        pltpu.make_async_copy(recv.at[c, pl.ds(gx * 2, 2)], there, out_l.at[c]).wait()
        return carry

    lax.fori_loop(0, chunks, finish, 0)
    rest = out.at[:, pl.ds(0, (nx - 1) * chunks)]
    pltpu.make_async_copy(rest, rest, out_r).wait()


def local(nx, ny, ensemble, obs_values, obs_error, tile_weight, owner_device, obs_cells):
    own, length, cols = ensemble.shape
    nb, nobs = obs_cells.shape
    members = own * nx
    rows = length // nx
    chunks = rows // CH
    dims = (nx, ny, members, rows, cols, nb, nobs)
    hbm = pl.BlockSpec(memory_space=pltpu.HBM)
    dma = pltpu.SemaphoreType.DMA
    tiles = ensemble.reshape(own, length // CH, CH, cols // 128, 128).transpose(0, 1, 3, 2, 4)
    result = pl.pallas_call(
        functools.partial(kernel, dims),
        out_shape=pltpu.VMEM(tiles.shape, F32),
        in_specs=[hbm] * 6,
        out_specs=pl.BlockSpec(memory_space=pl.ANY),
        scratch_shapes=[
            pltpu.SMEM((nb,), jnp.int32),
            pltpu.SMEM((nb, nobs), jnp.int32),
            pltpu.VMEM((nb, nobs), jnp.int32),
            pltpu.VMEM((nb, nobs), F32),
            pltpu.VMEM((nb, nobs), F32),
            pltpu.VMEM((nb, nobs), F32),
            pltpu.VMEM(tiles.shape, F32),
            pltpu.VMEM((chunks, members, cols // 128, CH, 128), F32),
            pltpu.VMEM((2, nb * nobs, 128), F32),
            pltpu.VMEM((16, nobs), F32),
            pltpu.VMEM((2 * ny, nobs), F32),
            pltpu.VMEM((ny, 2 * nx, nobs), F32),
            pltpu.VMEM((members, nb * nobs), F32),
            pltpu.VMEM((nb, nobs, 4 * members), BF16),
            pltpu.VMEM((nb, 2 * members, 2 * nobs), BF16),
            pltpu.VMEM((nb, nobs, cols), F32),
            pltpu.VMEM((nb, nobs, 128), F32),
            dma,
            dma,
            dma,
            dma,
            dma,
            dma,
            dma((chunks,)),
            dma((chunks,)),
            dma((chunks,)),
            dma((chunks,)),
            dma,
            dma((chunks,)),
            dma((7,)),
            pltpu.SemaphoreType.REGULAR,
            pltpu.SemaphoreType.REGULAR,
        ],
        compiler_params=pltpu.CompilerParams(
            collective_id=0, has_side_effects=True, vmem_limit_bytes=52 * 1024 * 1024
        ),
    )(
        owner_device,
        obs_cells,
        obs_values,
        obs_error,
        tile_weight.reshape(nb, nobs),
        tiles,
    )
    return result.transpose(0, 1, 3, 2, 4).reshape(ensemble.shape)


def solution(mesh):
    placed = (P("gx", None, "gy"), P(), P(), P(None, None, "gx", "gy"), P(), P())
    return jax.shard_map(
        functools.partial(local, mesh.shape["gx"], mesh.shape["gy"]),
        mesh=mesh,
        in_specs=placed,
        out_specs=P("gx", None, "gy"),
        check_vma=False,
    )
```
